32 devices in a mesh: parts: 2 (over x), seq: 16 (over z, y, core).
Axes of the slice: x: 2, y: 2, z: 4, core: 2. Of those that a mesh axis runs over, the one named last changes fastest.
Arguments:
- queries: bfloat16 [6144, 8, 128], P(('parts', 'seq')), parts along dimension 0, may hold values from -6 to 6
- key_rows: bfloat16 [6144, 8, 128], P(('parts', 'seq')), parts along dimension 0, may hold values from -6 to 6
- value_rows: bfloat16 [6144, 8, 128], P(('parts', 'seq')), parts along dimension 0, may hold values from -6 to 6
- grad_out: bfloat16 [6144, 8, 128], P(('parts', 'seq')), parts along dimension 0, may hold values from -6 to 6
- kv_tiles: int32 [96, 12], P('parts'), parts along dimension 0, may hold values from 0 to 47, as said below
- counts: int32 [96], P('parts'), parts along dimension 0, may hold values from 4 to 12, as said below
Outputs:
- attended: bfloat16 [6144, 8, 128], P(('parts', 'seq')), parts along dimension 0
- grad_queries: bfloat16 [6144, 8, 128], P(('parts', 'seq')), parts along dimension 0
- grad_keys: bfloat16 [6144, 8, 128], P(('parts', 'seq')), parts along dimension 0
- grad_values: bfloat16 [6144, 8, 128], P(('parts', 'seq')), parts along dimension 0
The draws below stay inside these ranges and needn't reach their ends.
There are 2 independent parts, one for each index of `parts`. The reference program is written for one: setup_inputs(seed, part) draws one part's arguments, and reference() takes and returns one part's arrays. A program takes and returns all parts, laid end to end along the dimension named above; each array names one. Nothing has to cross between parts.
Inputs may be any that keep to these rules, and one draw needn't show every extreme that they name: `kv_tiles`: tiles form frames of 4 rows of 3 tiles each, in order frame, row, column. Row i holds distinct tiles that differ from tile i by at most one in frame, row and column, the first being i itself, in its first counts[i] entries; the remaining entries equal i. counts[i] is at most the number of tiles within one frame, row and column of tile i; some tile has exactly 12.
All inputs are finite; a program needn't handle non-finite values.
Results may differ from the reference program's by a relative error of at most 0.018.
Values may be sent and summed in bfloat16 or wider, within the bound.
A program may use at most 128 MiB of HBM per device.

```python
import jax
import jax.numpy as jnp
from jax import lax

HEADS = 8
HEAD_DIM = 128
TILE = 64
NB = 12
TILES_DEV = 3
TILES = 48
TOKENS = 3072


def tile_lists(key):
    tile_ids = jnp.arange(TILES)
    frame_of = tile_ids // (4 * TILES_DEV)
    row_of = tile_ids // TILES_DEV % 4
    column_of = tile_ids % TILES_DEV
    near_frame = jnp.abs(frame_of[:, None] - frame_of[None, :]) <= 1
    near_row = jnp.abs(row_of[:, None] - row_of[None, :]) <= 1
    near_column = jnp.abs(column_of[:, None] - column_of[None, :]) <= 1
    nearby = (near_frame & near_row & near_column).astype(jnp.int32)
    itself = (tile_ids[:, None] == tile_ids[None, :]).astype(jnp.int32)
    noise = jax.random.randint(jax.random.fold_in(key, 101), (TILES, TILES), 0, 4096)
    ranking = ((itself * 2 + nearby) * 4096 + noise) * TILES + tile_ids[None, :]
    unused_vals, chosen = lax.top_k(ranking, NB)
    candidates = jnp.sum(nearby, axis=1)
    drawn = jax.random.randint(jax.random.fold_in(key, 102), (TILES,), NB // 3, NB + 1)
    live = jnp.minimum(drawn, candidates)
    frame_total = TILES // (4 * TILES_DEV)
    forced_frame = jax.random.randint(jax.random.fold_in(key, 103), (), 1, frame_total - 1)
    forced_tile = forced_frame * 4 * TILES_DEV + TILES_DEV + 1
    live = jnp.where(tile_ids == forced_tile, NB, live).astype(jnp.int32)
    slot_ids = jnp.arange(NB)
    lists = jnp.where(slot_ids[None, :] < live[:, None], chosen, tile_ids[:, None]).astype(jnp.int32)
    return (lists, live)


def draw_kv_tiles(key, part):
    lists, live = tile_lists(key)
    return lists


def draw_counts(key, part):
    lists, live = tile_lists(key)
    return live


def draw_queries(key, part):
    key = jax.random.fold_in(key, 3)
    shape_full = (TILES, TILE, HEADS, HEAD_DIM)
    drawn = jnp.clip(jax.random.normal(key, shape_full, jnp.float32), -6.0, 6.0)
    return drawn.reshape(TILES * TILE, HEADS, HEAD_DIM).astype(jnp.bfloat16)


def draw_key_rows(key, part):
    key = jax.random.fold_in(key, 4)
    shape_full = (TILES, TILE, HEADS, HEAD_DIM)
    drawn = jnp.clip(jax.random.normal(key, shape_full, jnp.float32), -6.0, 6.0)
    return drawn.reshape(TILES * TILE, HEADS, HEAD_DIM).astype(jnp.bfloat16)


def levels(key, dims, pieces, smallest, high):
    def one(axis_at, parts):
        draws = jax.random.uniform(jax.random.fold_in(jax.random.fold_in(key, 6), axis_at), (parts,), jnp.float32, smallest / len(pieces), high / len(pieces))
        return jnp.repeat(jnp.exp(draws), dims[axis_at] // parts).reshape((-1,) + (1,) * (len(dims) - axis_at - 1))

    gain = one(*pieces[0])
    for cut in pieces[1:]:
        gain = gain * one(*cut)
    return gain


def gaussian(own_key, shape, width, most, shards=(), dtype=jnp.bfloat16):
    factor_of = levels(own_key, shape, shards, -0.22, 0.18) if shards else 1.0
    array = jax.random.normal(own_key, shape, jnp.float32) * width * factor_of
    return jnp.minimum(jnp.maximum(array, -most), most).astype(dtype)


def setup_inputs(seed: int = 0, part: int = 0) -> dict:
    arg_keys = jax.random.split(jax.random.key(seed), 7)
    part_splits = jax.random.split(jax.random.fold_in(arg_keys[6], part), 7)
    queries = draw_queries(jax.random.fold_in(jax.random.fold_in(arg_keys[6], part), 71), part)
    key_rows = draw_key_rows(jax.random.fold_in(jax.random.fold_in(arg_keys[6], part), 71), part)
    value_rows = gaussian(part_splits[2], (TOKENS, HEADS, HEAD_DIM), 1.0, 6.0, ((0, 16),))
    grad_out = gaussian(part_splits[3], (TOKENS, HEADS, HEAD_DIM), 1.0, 6.0, ((0, 16),))
    kv_tiles = draw_kv_tiles(jax.random.fold_in(jax.random.fold_in(arg_keys[6], part), 71), part)
    counts = draw_counts(jax.random.fold_in(jax.random.fold_in(arg_keys[6], part), 71), part)
    return {"queries": queries, "key_rows": key_rows, "value_rows": value_rows, "grad_out": grad_out, "kv_tiles": kv_tiles, "counts": counts}


def reference(queries, key_rows, value_rows, grad_out, kv_tiles, counts):
    tile_count = kv_tiles.shape[0]
    list_len = kv_tiles.shape[1]
    scale_qk = HEAD_DIM ** -0.5
    shape_tiles = (tile_count, TILE, HEADS, HEAD_DIM)
    key_tiles = key_rows.reshape(shape_tiles)
    value_tiles = value_rows.reshape(shape_tiles)
    query_tiles = queries.reshape(shape_tiles)
    grad_tiles = grad_out.reshape(shape_tiles)

    def one_tile(carry, inputs):
        acc_keys, acc_values = carry
        query_one, grad_one, row_list, row_count = inputs
        keys_sel = jnp.take(key_tiles, row_list, axis=0).reshape(list_len * TILE, HEADS, HEAD_DIM).astype(jnp.float32)
        values_sel = jnp.take(value_tiles, row_list, axis=0).reshape(list_len * TILE, HEADS, HEAD_DIM).astype(jnp.float32)
        valid_keys = jnp.repeat(jnp.arange(list_len) < row_count, TILE)
        query_f = query_one.astype(jnp.float32)
        grad_f = grad_one.astype(jnp.float32)
        scores = jnp.einsum("qhd,khd->hqk", query_f, keys_sel) * scale_qk
        scores = jnp.where(valid_keys[None, None, :], scores, -jnp.inf)
        row_max = jnp.max(scores, axis=-1, keepdims=True)
        log_total = row_max + jnp.log(jnp.sum(jnp.exp(scores - row_max), axis=-1, keepdims=True))
        weights = lax.optimization_barrier(jnp.exp(scores - log_total).astype(jnp.bfloat16))
        weights_f = weights.astype(jnp.float32)
        attended = lax.optimization_barrier(jnp.einsum("hqk,khd->qhd", weights_f, values_sel).astype(jnp.bfloat16))
        grad_weights = jnp.einsum("qhd,khd->hqk", grad_f, values_sel)
        delta = jnp.transpose(jnp.sum(grad_f * attended.astype(jnp.float32), axis=-1))
        grad_scores = lax.optimization_barrier((weights_f * (grad_weights - delta[:, :, None]) * scale_qk).astype(jnp.bfloat16))
        grad_scores_f = grad_scores.astype(jnp.float32)
        grad_query = jnp.einsum("hqk,khd->qhd", grad_scores_f, keys_sel).astype(jnp.bfloat16)
        part_keys = jnp.einsum("hqk,qhd->khd", grad_scores_f, query_f).reshape(list_len, TILE, HEADS, HEAD_DIM)
        part_values = jnp.einsum("hqk,qhd->khd", weights_f, grad_f).reshape(list_len, TILE, HEADS, HEAD_DIM)
        acc_keys = acc_keys.at[row_list].add(part_keys)
        acc_values = acc_values.at[row_list].add(part_values)
        return (acc_keys, acc_values), (attended, grad_query)

    start = (jnp.zeros(shape_tiles, jnp.float32), jnp.zeros(shape_tiles, jnp.float32))
    (acc_keys, acc_values), (attended, grad_query) = lax.scan(one_tile, start, (query_tiles, grad_tiles, kv_tiles, counts))
    full_shape = queries.shape
    return (attended.reshape(full_shape), grad_query.reshape(full_shape),
            acc_keys.reshape(full_shape).astype(jnp.bfloat16), acc_values.reshape(full_shape).astype(jnp.bfloat16))
```

```python
import functools

import jax
import jax.numpy as jnp
from jax import lax
from jax.experimental import pallas as pl
from jax.experimental.pallas import tpu as pltpu
from jax.sharding import PartitionSpec as P

TILE = 64
ROWS = 4
MESH = pl.DeviceIdType.MESH
LOG2E = 1.4426950408889634
HIDE = -1e30
CENTRE = 4
KEYS, VALUES, QUERIES, GRADS = range(4)


def slot_of(frame_step, row_step):
    return (frame_step + 1) * 3 + row_step + 1


def dot(a, b, contract):
    return lax.dot_general(a, b, (((contract[0],), (contract[1],)), ((), ())), preferred_element_type=jnp.float32)


def kernel(devices, x_ref, kv_ref, out_ref, bank, stats, bias_q, bias_k, load_sem, send_sem, recv_sem, stat_send, stat_recv):
    heads, tok, dim = x_ref.shape[1:]
    cols = tok // TILE
    band = 9 * tok
    scale = dim ** -0.5
    me = lax.axis_index("seq")
    frame, row = me // ROWS, me % ROWS
    frames = devices // ROWS
    has_frame = {-1: frame > 0, 1: frame < frames - 1}
    has_row = {-1: row > 0, 1: row < ROWS - 1}
    crosses = {-1: row == 2, 1: row == 1}
    middle = (row == 1) | (row == 2)
    row_way = jnp.where(row == 1, 1, -1)

    def has(df, dr):
        cond = None
        if df:
            cond = has_frame[df]
        if dr:
            cond = has_row[dr] if cond is None else cond & has_row[dr]
        return cond

    around = [(df, dr) for df in (-1, 0, 1) for dr in (-1, 0, 1) if df or dr]

    load = pltpu.make_async_copy(x_ref, bank.at[:, :, CENTRE], load_sem)
    load.start()
    barrier = pltpu.get_barrier_semaphore()
    for df, dr in around:
        @pl.when(has(df, dr))
        def _():
            pl.semaphore_signal(barrier, inc=1, device_id={"seq": me + df * ROWS + dr}, device_id_type=MESH)
    frame_peers = jnp.where(has_frame[-1], 1, 0) + jnp.where(has_frame[1], 1, 0) + 1
    row_peers = jnp.where(has_row[-1], 1, 0) + jnp.where(has_row[1], 1, 0) + 1
    pl.semaphore_wait(barrier, frame_peers * row_peers - 1)

    def remote(g, h, src, dst, step, kind):
        c = g * heads + h
        return pltpu.make_async_remote_copy(
            src_ref=bank.at[pl.ds(2 * g, 2), h, src], dst_ref=bank.at[pl.ds(2 * g, 2), h, dst],
            send_sem=send_sem.at[kind, c], recv_sem=recv_sem.at[dst, c],
            device_id={"seq": me + step}, device_id_type=MESH)

    def wait_in(g, h, slot):
        c = g * heads + h
        part = bank.at[pl.ds(2 * g, 2), h, slot]
        pltpu.make_async_copy(part, part, recv_sem.at[slot, c]).wait()

    def frame_first(h):
        return h % 3 != 1

    def own_sends(g, h, act):
        for k, df in enumerate((-1, 1)):
            @pl.when(has_frame[df])
            def _():
                act(remote(g, h, CENTRE, slot_of(-df, 0), df * ROWS, k))
        for k, dr in enumerate((-1, 1)):
            @pl.when(has_row[dr])
            def _():
                act(remote(g, h, CENTRE, slot_of(0, -dr), dr, 2 + k))

    def later_sends(g, h, act, wait):
        kind = 4
        for df in (-1, 1):
            if wait:
                @pl.when(has_frame[df])
                def _():
                    wait_in(g, h, slot_of(df, 0))
            for dr in (-1, 1):
                @pl.when(has(df, dr) & (frame_first(h) | ~crosses[dr]))
                def _():
                    act(remote(g, h, slot_of(df, 0), slot_of(df, -dr), dr, kind))
                kind += 1
        if wait:
            @pl.when(middle & ~frame_first(h))
            def _():
                wait_in(g, h, CENTRE + row_way)
        for df in (-1, 1):
            @pl.when(has_frame[df] & middle & ~frame_first(h))
            def _():
                act(remote(g, h, CENTRE + row_way, (1 - df) * 3 + 1 + row_way, df * ROWS, kind))
            kind += 1

    def wait_rest(g, h):
        for dr in (-1, 1):
            @pl.when(has_row[dr] & (frame_first(h) | ~crosses[dr]))
            def _():
                wait_in(g, h, slot_of(0, dr))
        for df in (-1, 1):
            for dr in (-1, 1):
                @pl.when(has(df, dr))
                def _():
                    wait_in(g, h, slot_of(df, dr))

    def stat_copy(h, df, dr):
        dst = slot_of(-df, -dr)
        return pltpu.make_async_remote_copy(
            src_ref=stats.at[h, CENTRE], dst_ref=stats.at[h, dst],
            send_sem=stat_send.at[dst, h], recv_sem=stat_recv.at[dst, h],
            device_id={"seq": me + df * ROWS + dr}, device_id_type=MESH)

    def start(copy):
        copy.start()

    def wait_send(copy):
        copy.wait_send()

    load.wait()
    own_sends(0, 0, start)
    own_sends(0, 1, start)
    own_sends(1, 0, start)

    for df, dr in around:
        @pl.when(~has(df, dr))
        def _():
            slot = slot_of(df, dr)

            def clear(h, carry):
                for a in range(4):
                    bank[a, h, slot] = jnp.zeros((tok, dim), bank.dtype)
                stats[h, slot] = jnp.zeros(stats.shape[2:], stats.dtype)
                return carry

            lax.fori_loop(0, heads, clear, 0)

    tiles = kv_ref.shape[0]
    tile_ids = lax.broadcasted_iota(jnp.int32, (tiles, tiles), 1)
    listed = jnp.zeros((tiles, tiles), jnp.float32)
    for e in range(kv_ref.shape[1]):
        listed = jnp.where(kv_ref[:, e:e + 1] == tile_ids, 1.0, listed)
    lane = lax.broadcasted_iota(jnp.int32, (tiles, band), 1)
    slot_at = jnp.zeros_like(lane)
    for j in range(1, 9):
        slot_at += (lane >= j * tok).astype(jnp.int32)
    df_at = (lane >= 3 * tok).astype(jnp.int32) + (lane >= 6 * tok).astype(jnp.int32) - 1
    dr_at = slot_at - 3 * (df_at + 1) - 1
    col_at = lax.shift_right_logical(lane - slot_at * tok, 6)
    there = (frame + df_at >= 0) & (frame + df_at < frames) & (row + dr_at >= 0) & (row + dr_at < ROWS)
    tile_at = jnp.where(there, (me + df_at * ROWS + dr_at) * cols + col_at, -1)
    place = jnp.where(tile_at == lax.broadcasted_iota(jnp.int32, (tiles, band), 0), 1.0, 0.0)
    mine = jnp.where(
        lax.broadcasted_iota(jnp.int32, (8, tiles), 1) == me * cols + lax.broadcasted_iota(jnp.int32, (8, tiles), 0),
        1.0, 0.0)
    bias_q[...] = jnp.where(dot(dot(mine, listed, (1, 0)), place, (1, 0)) > 0.5, 0.0, HIDE)
    bias_k[...] = jnp.where(dot(dot(mine, listed, (1, 1)), place, (1, 0)) > 0.5, 0.0, HIDE)

    def rows_of(x, t):
        return x[t * TILE:(t + 1) * TILE]

    def queries_side(h):
        q, do = bank[QUERIES, h, CENTRE], bank[GRADS, h, CENTRE]
        k, v = bank[KEYS, h].reshape(band, dim), bank[VALUES, h].reshape(band, dim)
        s = dot(q, k, (1, 1))
        weights, tops, totals = [], [], []
        for t in range(cols):
            z = rows_of(s, t) * (scale * LOG2E) + bias_q[t:t + 1, :]
            top = jnp.max(z, axis=1, keepdims=True)
            w = jnp.exp2(z - top)
            weights.append(w)
            tops.append(top)
            totals.append(jnp.sum(w, axis=1, keepdims=True))
        w = jnp.concatenate(weights, axis=0)
        top, total = jnp.concatenate(tops, axis=0), jnp.concatenate(totals, axis=0)
        inv = 1.0 / total
        out = (dot(w.astype(jnp.bfloat16), v, (1, 0)) * inv).astype(jnp.bfloat16)
        out_ref[0, h] = out
        delta = jnp.sum(do.astype(jnp.float32) * out.astype(jnp.float32), axis=1, keepdims=True)
        dw = dot(do, v, (1, 1))
        ds = (w * (dw - delta) * (inv * scale)).astype(jnp.bfloat16)
        out_ref[1, h] = dot(ds, k, (1, 0)).astype(jnp.bfloat16)
        lse = top + jnp.log(total) * LOG2E
        wide = jnp.where(lax.broadcasted_iota(jnp.int32, (tok, 128), 1) == 0, lse, delta)
        turned = jnp.transpose(wide)
        stats[h, CENTRE, :, 0:tok] = turned[0:8]

    def keys_side(h):
        k, v = bank[KEYS, h, CENTRE], bank[VALUES, h, CENTRE]
        q, do = bank[QUERIES, h].reshape(band, dim), bank[GRADS, h].reshape(band, dim)
        s = dot(k, q, (1, 1))
        st = jnp.concatenate([stats[h, j, :, 0:tok] for j in range(9)], axis=1)
        lse, delta = st[0:1], st[1:2]
        w = jnp.concatenate(
            [jnp.exp2(rows_of(s, t) * (scale * LOG2E) + (bias_k[t:t + 1, :] - lse)) for t in range(cols)], axis=0)
        out_ref[3, h] = dot(w.astype(jnp.bfloat16), do, (1, 0)).astype(jnp.bfloat16)
        dw = dot(v, do, (1, 1))
        ds = (w * ((dw - delta) * scale)).astype(jnp.bfloat16)
        out_ref[2, h] = dot(ds, q, (1, 0)).astype(jnp.bfloat16)

    later_sends(0, 0, start, True)

    def step(i, carry):
        @pl.when(i + 2 < heads)
        def _():
            own_sends(0, i + 2, start)

        @pl.when(i + 1 < heads)
        def _():
            own_sends(1, i + 1, start)
            later_sends(0, i + 1, start, True)

        @pl.when(i < heads)
        def _():
            later_sends(1, i, start, True)
            wait_rest(0, i)
            queries_side(i)
            for df, dr in around:
                @pl.when(has(df, dr))
                def _():
                    stat_copy(i, df, dr).start()

        @pl.when(i >= 1)
        def _():
            wait_rest(1, i - 1)
            for df, dr in around:
                @pl.when(has(df, dr))
                def _():
                    slot = slot_of(df, dr)
                    part = stats.at[i - 1, slot]
                    pltpu.make_async_copy(part, part, stat_recv.at[slot, i - 1]).wait()
            keys_side(i - 1)

        return carry

    lax.fori_loop(0, heads + 1, step, 0)

    def finish(h, carry):
        for g in range(2):
            own_sends(g, h, wait_send)
            later_sends(g, h, wait_send, False)
        for df, dr in around:
            @pl.when(has(df, dr))
            def _():
                stat_copy(h, df, dr).wait_send()
        return carry

    lax.fori_loop(0, heads, finish, 0)


def on_device(devices, queries, key_rows, value_rows, grad_out, kv_tiles, counts):
    tok, heads, dim = queries.shape
    x = jnp.stack([key_rows, value_rows, queries, grad_out]).transpose(0, 2, 1, 3)
    out = pl.pallas_call(
        functools.partial(kernel, devices),
        out_shape=jax.ShapeDtypeStruct((4, heads, tok, dim), jnp.bfloat16),
        in_specs=[pl.BlockSpec(memory_space=pl.ANY), pl.BlockSpec(memory_space=pltpu.VMEM)],
        out_specs=pl.BlockSpec(memory_space=pltpu.VMEM),
        scratch_shapes=[
            pltpu.VMEM((4, heads, 9, tok, dim), jnp.bfloat16),
            pltpu.VMEM((heads, 9, 8, 256), jnp.float32),
            pltpu.VMEM((8, 9 * tok), jnp.float32),
            pltpu.VMEM((8, 9 * tok), jnp.float32),
            pltpu.SemaphoreType.DMA,
            pltpu.SemaphoreType.DMA((10, 2 * heads)),
            pltpu.SemaphoreType.DMA((9, 2 * heads)),
            pltpu.SemaphoreType.DMA((9, heads)),
            pltpu.SemaphoreType.DMA((9, heads)),
        ],
        compiler_params=pltpu.CompilerParams(collective_id=0, has_side_effects=True, vmem_limit_bytes=56 * 2**20),
    )(x, kv_tiles)
    out = out.transpose(0, 2, 1, 3)
    return (out[0], out[1], out[2], out[3])


def solution(mesh):
    rows = P(("parts", "seq"), None, None)
    return jax.shard_map(
        functools.partial(on_device, mesh.shape["seq"]),
        mesh=mesh,
        in_specs=(rows, rows, rows, rows, P("parts", None), P("parts")),
        out_specs=(rows, rows, rows, rows),
        check_vma=False,
    )
```

```python
import functools

import jax
import jax.numpy as jnp
from jax import lax
from jax.experimental import pallas as pl
from jax.experimental.pallas import tpu as pltpu
from jax.sharding import PartitionSpec as P

TILE = 64
ROWS = 4
MESH = pl.DeviceIdType.MESH
LOG2E = 1.4426950408889634
HIDE = -1e30
CENTRE = 4
OWN_AHEAD, PASS_AHEAD, LAG = 4, 2, 2
KEYS, VALUES, QUERIES, GRADS = range(4)


def slot_of(frame_step, row_step):
    return (frame_step + 1) * 3 + row_step + 1


def dot(a, b, contract):
    return lax.dot_general(a, b, (((contract[0],), (contract[1],)), ((), ())), preferred_element_type=jnp.float32)


def kernel(devices, k_ref, v_ref, q_ref, do_ref, kv_ref, out_ref, bank, stats, bias_q, bias_k, send_sem, recv_sem, stat_send, stat_recv):
    tok, heads, dim = q_ref.shape
    cols = tok // TILE
    band = 9 * tok
    scale = dim ** -0.5
    me = lax.axis_index("seq")
    frame, row = me // ROWS, me % ROWS
    frames = devices // ROWS
    has_frame = {-1: frame > 0, 1: frame < frames - 1}
    has_row = {-1: row > 0, 1: row < ROWS - 1}
    crosses = {-1: row == 2, 1: row == 1}
    middle = (row == 1) | (row == 2)
    row_way = jnp.where(row == 1, 1, -1)

    def has(df, dr):
        cond = None
        if df:
            cond = has_frame[df]
        if dr:
            cond = has_row[dr] if cond is None else cond & has_row[dr]
        return cond

    around = [(df, dr) for df in (-1, 0, 1) for dr in (-1, 0, 1) if df or dr]

    barrier = pltpu.get_barrier_semaphore()
    for df, dr in around:
        @pl.when(has(df, dr))
        def _():
            pl.semaphore_signal(barrier, inc=1, device_id={"seq": me + df * ROWS + dr}, device_id_type=MESH)
    frame_peers = jnp.where(has_frame[-1], 1, 0) + jnp.where(has_frame[1], 1, 0) + 1
    row_peers = jnp.where(has_row[-1], 1, 0) + jnp.where(has_row[1], 1, 0) + 1
    for a, ref in enumerate((k_ref, v_ref, q_ref, do_ref)):
        bank[a, :, CENTRE] = jnp.transpose(ref[...], (1, 0, 2))
    pl.semaphore_wait(barrier, frame_peers * row_peers - 1)

    def remote(g, h, src, dst, step, kind):
        c = g * heads + h
        return pltpu.make_async_remote_copy(
            src_ref=bank.at[pl.ds(2 * g, 2), h, src], dst_ref=bank.at[pl.ds(2 * g, 2), h, dst],
            send_sem=send_sem.at[kind, c], recv_sem=recv_sem.at[dst, c],
            device_id={"seq": me + step}, device_id_type=MESH)

    def wait_in(g, h, slot):
        c = g * heads + h
        part = bank.at[pl.ds(2 * g, 2), h, slot]
        pltpu.make_async_copy(part, part, recv_sem.at[slot, c]).wait()

    def frame_first(h):
        return h % 3 != 1

    def own_sends(g, h, act):
        for k, df in enumerate((-1, 1)):
            @pl.when(has_frame[df])
            def _():
                act(remote(g, h, CENTRE, slot_of(-df, 0), df * ROWS, k))
        for k, dr in enumerate((-1, 1)):
            @pl.when(has_row[dr])
            def _():
                act(remote(g, h, CENTRE, slot_of(0, -dr), dr, 2 + k))

    def later_sends(g, h, act, wait):
        kind = 4
        for df in (-1, 1):
            if wait:
                @pl.when(has_frame[df])
                def _():
                    wait_in(g, h, slot_of(df, 0))
            for dr in (-1, 1):
                @pl.when(has(df, dr) & (frame_first(h) | ~crosses[dr]))
                def _():
                    act(remote(g, h, slot_of(df, 0), slot_of(df, -dr), dr, kind))
                kind += 1
        if wait:
            @pl.when(middle & ~frame_first(h))
            def _():
                wait_in(g, h, CENTRE + row_way)
        for df in (-1, 1):
            @pl.when(has_frame[df] & middle & ~frame_first(h))
            def _():
                act(remote(g, h, CENTRE + row_way, (1 - df) * 3 + 1 + row_way, df * ROWS, kind))
            kind += 1

    def wait_rest(g, h):
        for dr in (-1, 1):
            @pl.when(has_row[dr] & (frame_first(h) | ~crosses[dr]))
            def _():
                wait_in(g, h, slot_of(0, dr))
        for df in (-1, 1):
            for dr in (-1, 1):
                @pl.when(has(df, dr))
                def _():
                    wait_in(g, h, slot_of(df, dr))

    def stat_copy(h, df, dr):
        dst = slot_of(-df, -dr)
        return pltpu.make_async_remote_copy(
            src_ref=stats.at[h, CENTRE], dst_ref=stats.at[h, dst],
            send_sem=stat_send.at[dst, h], recv_sem=stat_recv.at[dst, h],
            device_id={"seq": me + df * ROWS + dr}, device_id_type=MESH)

    def start(copy):
        copy.start()

    def wait_send(copy):
        copy.wait_send()

    for lead in range(OWN_AHEAD - PASS_AHEAD):
        own_sends(0, lead, start)
        if lead >= LAG:
            own_sends(1, lead - LAG, start)

    for df, dr in around:
        @pl.when(~has(df, dr))
        def _():
            slot = slot_of(df, dr)

            def clear(h, carry):
                for a in range(4):
                    bank[a, h, slot] = jnp.zeros((tok, dim), bank.dtype)
                stats[h, slot] = jnp.zeros(stats.shape[2:], stats.dtype)
                return carry

            lax.fori_loop(0, heads, clear, 0)

    tiles = kv_ref.shape[1]
    tile_ids = lax.broadcasted_iota(jnp.int32, (tiles, tiles), 0)
    listed = jnp.zeros((tiles, tiles), jnp.float32)
    for e in range(kv_ref.shape[0]):
        listed = jnp.where(kv_ref[e:e + 1, :] == tile_ids, 1.0, listed)
    lane = lax.broadcasted_iota(jnp.int32, (tiles, band), 1)
    slot_at = jnp.zeros_like(lane)
    for j in range(1, 9):
        slot_at += (lane >= j * tok).astype(jnp.int32)
    df_at = (lane >= 3 * tok).astype(jnp.int32) + (lane >= 6 * tok).astype(jnp.int32) - 1
    dr_at = slot_at - 3 * (df_at + 1) - 1
    col_at = lax.shift_right_logical(lane - slot_at * tok, 6)
    there = (frame + df_at >= 0) & (frame + df_at < frames) & (row + dr_at >= 0) & (row + dr_at < ROWS)
    tile_at = jnp.where(there, (me + df_at * ROWS + dr_at) * cols + col_at, -1)
    place = jnp.where(tile_at == lax.broadcasted_iota(jnp.int32, (tiles, band), 0), 1.0, 0.0)
    mine = jnp.where(
        lax.broadcasted_iota(jnp.int32, (8, tiles), 1) == me * cols + lax.broadcasted_iota(jnp.int32, (8, tiles), 0),
        1.0, 0.0)
    bias_q[...] = jnp.where(dot(dot(mine, listed, (1, 1)), place, (1, 0)) > 0.5, 0.0, HIDE)
    bias_k[...] = jnp.where(dot(dot(mine, listed, (1, 0)), place, (1, 0)) > 0.5, 0.0, HIDE)

    def rows_of(x, t):
        return x[t * TILE:(t + 1) * TILE]

    def queries_side(h):
        q, do = bank[QUERIES, h, CENTRE], bank[GRADS, h, CENTRE]
        k, v = bank[KEYS, h].reshape(band, dim), bank[VALUES, h].reshape(band, dim)
        s = dot(q, k, (1, 1))
        weights, tops, totals = [], [], []
        for t in range(cols):
            z = rows_of(s, t) * (scale * LOG2E) + bias_q[t:t + 1, :]
            top = jnp.max(z, axis=1, keepdims=True)
            w = jnp.exp2(z - top)
            weights.append(w)
            tops.append(top)
            totals.append(jnp.sum(w, axis=1, keepdims=True))
        w = jnp.concatenate(weights, axis=0)
        top, total = jnp.concatenate(tops, axis=0), jnp.concatenate(totals, axis=0)
        inv = 1.0 / total
        out = (dot(w.astype(jnp.bfloat16), v, (1, 0)) * inv).astype(jnp.bfloat16)
        out_ref[0, h] = out
        delta = jnp.sum(do.astype(jnp.float32) * out.astype(jnp.float32), axis=1, keepdims=True)
        dw = dot(do, v, (1, 1))
        ds = (w * (dw - delta) * (inv * scale)).astype(jnp.bfloat16)
        out_ref[1, h] = dot(ds, k, (1, 0)).astype(jnp.bfloat16)
        lse = top + jnp.log(total) * LOG2E
        wide = jnp.where(lax.broadcasted_iota(jnp.int32, (tok, 128), 1) == 0, lse, delta)
        turned = jnp.transpose(wide)
        stats[h, CENTRE, :, 0:tok] = turned[0:8]

    def keys_side(h):
        k, v = bank[KEYS, h, CENTRE], bank[VALUES, h, CENTRE]
        q, do = bank[QUERIES, h].reshape(band, dim), bank[GRADS, h].reshape(band, dim)
        s = dot(k, q, (1, 1))
        st = jnp.concatenate([stats[h, j, :, 0:tok] for j in range(9)], axis=1)
        lse, delta = st[0:1], st[1:2]
        w = jnp.concatenate(
            [jnp.exp2(rows_of(s, t) * (scale * LOG2E) + (bias_k[t:t + 1, :] - lse)) for t in range(cols)], axis=0)
        out_ref[3, h] = dot(w.astype(jnp.bfloat16), do, (1, 0)).astype(jnp.bfloat16)
        dw = dot(v, do, (1, 1))
        ds = (w * ((dw - delta) * scale)).astype(jnp.bfloat16)
        out_ref[2, h] = dot(ds, q, (1, 0)).astype(jnp.bfloat16)

    def step(t, carry):
        def at(lag):
            h = t - lag
            if lag > 0:
                return h, (h >= 0) & (h < heads)
            return h, h < heads

        h_own, turn = at(PASS_AHEAD - OWN_AHEAD)
        @pl.when(turn)
        def _():
            own_sends(0, h_own, start)

        h_own_late, turn = at(PASS_AHEAD - OWN_AHEAD + LAG)
        @pl.when(turn)
        def _():
            own_sends(1, h_own_late, start)

        h_pass, turn = at(0)
        @pl.when(turn)
        def _():
            later_sends(0, h_pass, start, True)

        h_pass_late, turn = at(LAG)
        @pl.when(turn)
        def _():
            later_sends(1, h_pass_late, start, True)

        i, turn = at(PASS_AHEAD)
        @pl.when(turn)
        def _():
            wait_rest(0, i)
            queries_side(i)
            for df, dr in around:
                @pl.when(has(df, dr))
                def _():
                    stat_copy(i, df, dr).start()

        h, turn = at(PASS_AHEAD + LAG)
        @pl.when(turn)
        def _():
            wait_rest(1, h)
            for df, dr in around:
                @pl.when(has(df, dr))
                def _():
                    slot = slot_of(df, dr)
                    part = stats.at[h, slot]
                    pltpu.make_async_copy(part, part, stat_recv.at[slot, h]).wait()
            keys_side(h)

        return carry

    lax.fori_loop(0, heads + LAG + PASS_AHEAD, step, 0)

    def finish(h, carry):
        for g in range(2):
            own_sends(g, h, wait_send)
            later_sends(g, h, wait_send, False)
        for df, dr in around:
            @pl.when(has(df, dr))
            def _():
                stat_copy(h, df, dr).wait_send()
        return carry

    lax.fori_loop(0, heads, finish, 0)


def by_token(in_ref, *out_refs):
    for a, ref in enumerate(out_refs):
        ref[...] = jnp.transpose(in_ref[a], (1, 0, 2))


def on_device(devices, queries, key_rows, value_rows, grad_out, kv_tiles, counts):
    tok, heads, dim = queries.shape
    out = pl.pallas_call(
        functools.partial(kernel, devices),
        out_shape=jax.ShapeDtypeStruct((4, heads, tok, dim), jnp.bfloat16),
        in_specs=[pl.BlockSpec(memory_space=pltpu.VMEM)] * 5,
        out_specs=pl.BlockSpec(memory_space=pltpu.VMEM),
        scratch_shapes=[
            pltpu.VMEM((4, heads, 9, tok, dim), jnp.bfloat16),
            pltpu.VMEM((heads, 9, 8, 256), jnp.float32),
            pltpu.VMEM((8, 9 * tok), jnp.float32),
            pltpu.VMEM((8, 9 * tok), jnp.float32),
            pltpu.SemaphoreType.DMA((10, 2 * heads)),
            pltpu.SemaphoreType.DMA((9, 2 * heads)),
            pltpu.SemaphoreType.DMA((9, heads)),
            pltpu.SemaphoreType.DMA((9, heads)),
        ],
        compiler_params=pltpu.CompilerParams(collective_id=0, has_side_effects=True, vmem_limit_bytes=56 * 2**20),
    )(key_rows, value_rows, queries, grad_out, kv_tiles.T)
    return tuple(pl.pallas_call(
        by_token,
        out_shape=[jax.ShapeDtypeStruct(queries.shape, queries.dtype)] * 4,
        in_specs=[pl.BlockSpec(memory_space=pltpu.VMEM)],
        out_specs=[pl.BlockSpec(memory_space=pltpu.VMEM)] * 4,
    )(out))


def solution(mesh):
    rows = P(("parts", "seq"), None, None)
    return jax.shard_map(
        functools.partial(on_device, mesh.shape["seq"]),
        mesh=mesh,
        in_specs=(rows, rows, rows, rows, P("parts", None), P("parts")),
        out_specs=(rows, rows, rows, rows),
        check_vma=False,
    )
```

```python
import functools

import jax
import jax.numpy as jnp
from jax import lax
from jax.experimental import pallas as pl
from jax.experimental.pallas import tpu as pltpu
from jax.sharding import PartitionSpec as P

TILE = 64
ROWS = 4
MESH = pl.DeviceIdType.MESH
LOG2E = 1.4426950408889634
HIDE = -1e30
CENTRE = 4
OWN_AHEAD, PASS_AHEAD, LAG = 4, 2, 2
KEYS, VALUES, QUERIES, GRADS = range(4)


def slot_of(frame_step, row_step):
    return (frame_step + 1) * 3 + row_step + 1


def dot(a, b, contract):
    return lax.dot_general(a, b, (((contract[0],), (contract[1],)), ((), ())), preferred_element_type=jnp.float32)


def kernel(devices, k_ref, v_ref, q_ref, do_ref, kv_ref, out_ref, bank, stats, bias_q, bias_k, send_sem, recv_sem, stat_send, stat_recv):
    tok, heads, dim = q_ref.shape
    cols = tok // TILE
    band = 9 * tok
    scale = dim ** -0.5
    me = lax.axis_index("seq")
    frame, row = me // ROWS, me % ROWS
    frames = devices // ROWS
    has_frame = {-1: frame > 0, 1: frame < frames - 1}
    has_row = {-1: row > 0, 1: row < ROWS - 1}
    crosses = {-1: row == 2, 1: row == 1}
    middle = (row == 1) | (row == 2)
    row_way = jnp.where(row == 1, 1, -1)

    def has(df, dr):
        cond = None
        if df:
            cond = has_frame[df]
        if dr:
            cond = has_row[dr] if cond is None else cond & has_row[dr]
        return cond

    around = [(df, dr) for df in (-1, 0, 1) for dr in (-1, 0, 1) if df or dr]

    barrier = pltpu.get_barrier_semaphore()
    for df, dr in around:
        @pl.when(has(df, dr))
        def _():
            pl.semaphore_signal(barrier, inc=1, device_id={"seq": me + df * ROWS + dr}, device_id_type=MESH)
    frame_peers = jnp.where(has_frame[-1], 1, 0) + jnp.where(has_frame[1], 1, 0) + 1
    row_peers = jnp.where(has_row[-1], 1, 0) + jnp.where(has_row[1], 1, 0) + 1
    bank[KEYS, :, CENTRE] = jnp.transpose(k_ref[...], (1, 0, 2))
    bank[VALUES, :, CENTRE] = jnp.transpose(v_ref[...], (1, 0, 2))
    pl.semaphore_wait(barrier, frame_peers * row_peers - 1)

    def remote(g, h, src, dst, step, kind):
        c = g * heads + h
        return pltpu.make_async_remote_copy(
            src_ref=bank.at[pl.ds(2 * g, 2), h, src], dst_ref=bank.at[pl.ds(2 * g, 2), h, dst],
            send_sem=send_sem.at[kind, c], recv_sem=recv_sem.at[dst, c],
            device_id={"seq": me + step}, device_id_type=MESH)

    def wait_in(g, h, slot):
        c = g * heads + h
        part = bank.at[pl.ds(2 * g, 2), h, slot]
        pltpu.make_async_copy(part, part, recv_sem.at[slot, c]).wait()

    def frame_first(h):
        return (h % 2 == 0) | (h < 2)

    def own_sends(g, h, act):
        for k, df in enumerate((-1, 1)):
            @pl.when(has_frame[df])
            def _():
                act(remote(g, h, CENTRE, slot_of(-df, 0), df * ROWS, k))
        for k, dr in enumerate((-1, 1)):
            @pl.when(has_row[dr] & (frame_first(h) | ~crosses[dr]))
            def _():
                act(remote(g, h, CENTRE, slot_of(0, -dr), dr, 2 + k))

    def crossing_sends(g, h, act):
        for k, dr in enumerate((-1, 1)):
            @pl.when(crosses[dr] & ~frame_first(h))
            def _():
                act(remote(g, h, CENTRE, slot_of(0, -dr), dr, 2 + k))

    def later_sends(g, h, act, wait):
        kind = 4
        for df in (-1, 1):
            if wait:
                @pl.when(has_frame[df])
                def _():
                    wait_in(g, h, slot_of(df, 0))
            for dr in (-1, 1):
                @pl.when(has(df, dr) & (frame_first(h) | ~crosses[dr]))
                def _():
                    act(remote(g, h, slot_of(df, 0), slot_of(df, -dr), dr, kind))
                kind += 1
        if wait:
            @pl.when(middle & ~frame_first(h))
            def _():
                wait_in(g, h, CENTRE + row_way)
        for df in (-1, 1):
            @pl.when(has_frame[df] & middle & ~frame_first(h))
            def _():
                act(remote(g, h, CENTRE + row_way, (1 - df) * 3 + 1 + row_way, df * ROWS, kind))
            kind += 1

    def wait_rest(g, h):
        for dr in (-1, 1):
            @pl.when(has_row[dr] & (frame_first(h) | ~crosses[dr]))
            def _():
                wait_in(g, h, slot_of(0, dr))
        for df in (-1, 1):
            for dr in (-1, 1):
                @pl.when(has(df, dr))
                def _():
                    wait_in(g, h, slot_of(df, dr))

    def stat_copy(h, df, dr):
        dst = slot_of(-df, -dr)
        return pltpu.make_async_remote_copy(
            src_ref=stats.at[h, CENTRE], dst_ref=stats.at[h, dst],
            send_sem=stat_send.at[dst, h], recv_sem=stat_recv.at[dst, h],
            device_id={"seq": me + df * ROWS + dr}, device_id_type=MESH)

    def start(copy):
        copy.start()

    def wait_send(copy):
        copy.wait_send()

    for lead in range(OWN_AHEAD - PASS_AHEAD):
        own_sends(0, lead, start)
    bank[QUERIES, :, CENTRE] = jnp.transpose(q_ref[...], (1, 0, 2))
    bank[GRADS, :, CENTRE] = jnp.transpose(do_ref[...], (1, 0, 2))

    def cross(h, carry):
        crossing_sends(0, h, start)
        crossing_sends(1, h, start)
        return carry

    lax.fori_loop(0, heads, cross, 0)

    for df, dr in around:
        @pl.when(~has(df, dr))
        def _():
            slot = slot_of(df, dr)

            def clear(h, carry):
                for a in range(4):
                    bank[a, h, slot] = jnp.zeros((tok, dim), bank.dtype)
                stats[h, slot] = jnp.zeros(stats.shape[2:], stats.dtype)
                return carry

            lax.fori_loop(0, heads, clear, 0)

    tiles = kv_ref.shape[1]
    tile_ids = lax.broadcasted_iota(jnp.int32, (tiles, tiles), 0)
    listed = jnp.zeros((tiles, tiles), jnp.float32)
    for e in range(kv_ref.shape[0]):
        listed = jnp.where(kv_ref[e:e + 1, :] == tile_ids, 1.0, listed)
    lane = lax.broadcasted_iota(jnp.int32, (tiles, band), 1)
    slot_at = jnp.zeros_like(lane)
    for j in range(1, 9):
        slot_at += (lane >= j * tok).astype(jnp.int32)
    df_at = (lane >= 3 * tok).astype(jnp.int32) + (lane >= 6 * tok).astype(jnp.int32) - 1
    dr_at = slot_at - 3 * (df_at + 1) - 1
    col_at = lax.shift_right_logical(lane - slot_at * tok, 6)
    there = (frame + df_at >= 0) & (frame + df_at < frames) & (row + dr_at >= 0) & (row + dr_at < ROWS)
    tile_at = jnp.where(there, (me + df_at * ROWS + dr_at) * cols + col_at, -1)
    place = jnp.where(tile_at == lax.broadcasted_iota(jnp.int32, (tiles, band), 0), 1.0, 0.0)
    mine = jnp.where(
        lax.broadcasted_iota(jnp.int32, (8, tiles), 1) == me * cols + lax.broadcasted_iota(jnp.int32, (8, tiles), 0),
        1.0, 0.0)
    bias_q[...] = jnp.where(dot(dot(mine, listed, (1, 1)), place, (1, 0)) > 0.5, 0.0, HIDE)
    bias_k[...] = jnp.where(dot(dot(mine, listed, (1, 0)), place, (1, 0)) > 0.5, 0.0, HIDE)

    def rows_of(x, t):
        return x[t * TILE:(t + 1) * TILE]

    def queries_side(h):
        q, do = bank[QUERIES, h, CENTRE], bank[GRADS, h, CENTRE]
        k, v = bank[KEYS, h].reshape(band, dim), bank[VALUES, h].reshape(band, dim)
        s = dot(q, k, (1, 1))
        weights, tops, totals = [], [], []
        for t in range(cols):
            z = rows_of(s, t) * (scale * LOG2E) + bias_q[t:t + 1, :]
            top = jnp.max(z, axis=1, keepdims=True)
            w = jnp.exp2(z - top)
            weights.append(w)
            tops.append(top)
            totals.append(jnp.sum(w, axis=1, keepdims=True))
        w = jnp.concatenate(weights, axis=0)
        top, total = jnp.concatenate(tops, axis=0), jnp.concatenate(totals, axis=0)
        inv = 1.0 / total
        out = (dot(w.astype(jnp.bfloat16), v, (1, 0)) * inv).astype(jnp.bfloat16)
        out_ref[0, h] = out
        delta = jnp.sum(do.astype(jnp.float32) * out.astype(jnp.float32), axis=1, keepdims=True)
        dw = dot(do, v, (1, 1))
        ds = (w * (dw - delta) * (inv * scale)).astype(jnp.bfloat16)
        out_ref[1, h] = dot(ds, k, (1, 0)).astype(jnp.bfloat16)
        lse = top + jnp.log(total) * LOG2E
        wide = jnp.where(lax.broadcasted_iota(jnp.int32, (tok, 128), 1) == 0, lse, delta)
        turned = jnp.transpose(wide)
        stats[h, CENTRE, :, 0:tok] = turned[0:2]

    def keys_side(h):
        k, v = bank[KEYS, h, CENTRE], bank[VALUES, h, CENTRE]
        q, do = bank[QUERIES, h].reshape(band, dim), bank[GRADS, h].reshape(band, dim)
        s = dot(k, q, (1, 1))
        st = jnp.concatenate([stats[h, j, :, 0:tok] for j in range(9)], axis=1)
        lse, delta = st[0:1], st[1:2]
        w = jnp.concatenate(
            [jnp.exp2(rows_of(s, t) * (scale * LOG2E) + (bias_k[t:t + 1, :] - lse)) for t in range(cols)], axis=0)
        out_ref[3, h] = dot(w.astype(jnp.bfloat16), do, (1, 0)).astype(jnp.bfloat16)
        dw = dot(v, do, (1, 1))
        ds = (w * ((dw - delta) * scale)).astype(jnp.bfloat16)
        out_ref[2, h] = dot(ds, q, (1, 0)).astype(jnp.bfloat16)

    def step(t, carry):
        def at(lag):
            h = t - lag
            if lag > 0:
                return h, (h >= 0) & (h < heads)
            return h, h < heads

        h_own, turn = at(PASS_AHEAD - OWN_AHEAD)
        @pl.when(turn)
        def _():
            own_sends(0, h_own, start)

        h_own_late, turn = at(PASS_AHEAD - OWN_AHEAD + LAG)
        @pl.when(turn)
        def _():
            own_sends(1, h_own_late, start)

        h_pass, turn = at(0)
        @pl.when(turn)
        def _():
            later_sends(0, h_pass, start, True)

        h_pass_late, turn = at(LAG)
        @pl.when(turn)
        def _():
            later_sends(1, h_pass_late, start, True)

        i, turn = at(PASS_AHEAD)
        @pl.when(turn)
        def _():
            wait_rest(0, i)
            queries_side(i)
            for df, dr in around:
                @pl.when(has(df, dr))
                def _():
                    stat_copy(i, df, dr).start()

        h, turn = at(PASS_AHEAD + LAG)
        @pl.when(turn)
        def _():
            wait_rest(1, h)
            for df, dr in around:
                @pl.when(has(df, dr))
                def _():
                    slot = slot_of(df, dr)
                    part = stats.at[h, slot]
                    pltpu.make_async_copy(part, part, stat_recv.at[slot, h]).wait()
            keys_side(h)

        return carry

    lax.fori_loop(0, heads + LAG + PASS_AHEAD, step, 0)

    def finish(h, carry):
        for g in range(2):
            own_sends(g, h, wait_send)
            crossing_sends(g, h, wait_send)
            later_sends(g, h, wait_send, False)
        for df, dr in around:
            @pl.when(has(df, dr))
            def _():
                stat_copy(h, df, dr).wait_send()
        return carry

    lax.fori_loop(0, heads, finish, 0)


def by_token(in_ref, *out_refs):
    for a, ref in enumerate(out_refs):
        ref[...] = jnp.transpose(in_ref[a], (1, 0, 2))


def on_device(devices, queries, key_rows, value_rows, grad_out, kv_tiles, counts):
    tok, heads, dim = queries.shape
    out = pl.pallas_call(
        functools.partial(kernel, devices),
        out_shape=jax.ShapeDtypeStruct((4, heads, tok, dim), jnp.bfloat16),
        in_specs=[pl.BlockSpec(memory_space=pltpu.VMEM)] * 5,
        out_specs=pl.BlockSpec(memory_space=pltpu.VMEM),
        scratch_shapes=[
            pltpu.VMEM((4, heads, 9, tok, dim), jnp.bfloat16),
            pltpu.VMEM((heads, 9, 2, 256), jnp.float32),
            pltpu.VMEM((8, 9 * tok), jnp.float32),
            pltpu.VMEM((8, 9 * tok), jnp.float32),
            pltpu.SemaphoreType.DMA((10, 2 * heads)),
            pltpu.SemaphoreType.DMA((9, 2 * heads)),
            pltpu.SemaphoreType.DMA((9, heads)),
            pltpu.SemaphoreType.DMA((9, heads)),
        ],
        compiler_params=pltpu.CompilerParams(collective_id=0, has_side_effects=True, vmem_limit_bytes=56 * 2**20),
    )(key_rows, value_rows, queries, grad_out, kv_tiles.T)
    return tuple(pl.pallas_call(
        by_token,
        out_shape=[jax.ShapeDtypeStruct(queries.shape, queries.dtype)] * 4,
        in_specs=[pl.BlockSpec(memory_space=pltpu.VMEM)],
        out_specs=[pl.BlockSpec(memory_space=pltpu.VMEM)] * 4,
    )(out))


def solution(mesh):
    rows = P(("parts", "seq"), None, None)
    return jax.shard_map(
        functools.partial(on_device, mesh.shape["seq"]),
        mesh=mesh,
        in_specs=(rows, rows, rows, rows, P("parts", None), P("parts")),
        out_specs=(rows, rows, rows, rows),
        check_vma=False,
    )
```

```python
import functools

import jax
import jax.numpy as jnp
from jax import lax
from jax.experimental import pallas as pl
from jax.experimental.pallas import tpu as pltpu
from jax.sharding import PartitionSpec as P

TILE = 64
ROWS = 4
MESH = pl.DeviceIdType.MESH
LOG2E = 1.4426950408889634
HIDE = -1e30
CENTRE = 4
OWN_AHEAD, PASS_AHEAD, LAG = 4, 2, 2
KEYS, VALUES, QUERIES, GRADS = range(4)


def slot_of(frame_step, row_step):
    return (frame_step + 1) * 3 + row_step + 1


def dot(a, b, contract):
    return lax.dot_general(a, b, (((contract[0],), (contract[1],)), ((), ())), preferred_element_type=jnp.float32)


def kernel(devices, k_ref, v_ref, q_ref, do_ref, kv_ref, out_ref, bank, stats, bias_q, bias_k, send_sem, recv_sem, stat_send, stat_recv):
    tok, heads, dim = q_ref.shape
    cols = tok // TILE
    band = 9 * tok
    scale = dim ** -0.5
    me = lax.axis_index("seq")
    frame, row = me // ROWS, me % ROWS
    frames = devices // ROWS
    has_frame = {-1: frame > 0, 1: frame < frames - 1}
    has_row = {-1: row > 0, 1: row < ROWS - 1}
    crosses = {-1: row == 2, 1: row == 1}
    middle = (row == 1) | (row == 2)
    row_way = jnp.where(row == 1, 1, -1)

    def has(df, dr):
        cond = None
        if df:
            cond = has_frame[df]
        if dr:
            cond = has_row[dr] if cond is None else cond & has_row[dr]
        return cond

    around = [(df, dr) for df in (-1, 0, 1) for dr in (-1, 0, 1) if df or dr]

    barrier = pltpu.get_barrier_semaphore()
    for df, dr in around:
        @pl.when(has(df, dr))
        def _():
            pl.semaphore_signal(barrier, inc=1, device_id={"seq": me + df * ROWS + dr}, device_id_type=MESH)
    frame_peers = jnp.where(has_frame[-1], 1, 0) + jnp.where(has_frame[1], 1, 0) + 1
    row_peers = jnp.where(has_row[-1], 1, 0) + jnp.where(has_row[1], 1, 0) + 1
    bank[KEYS, :, CENTRE] = jnp.transpose(k_ref[...], (1, 0, 2))
    bank[VALUES, :, CENTRE] = jnp.transpose(v_ref[...], (1, 0, 2))
    pl.semaphore_wait(barrier, frame_peers * row_peers - 1)

    def remote(g, h, src, dst, step, kind):
        c = g * heads + h
        return pltpu.make_async_remote_copy(
            src_ref=bank.at[pl.ds(2 * g, 2), h, src], dst_ref=bank.at[pl.ds(2 * g, 2), h, dst],
            send_sem=send_sem.at[kind, c], recv_sem=recv_sem.at[dst, c],
            device_id={"seq": me + step}, device_id_type=MESH)

    def wait_in(g, h, slot):
        c = g * heads + h
        part = bank.at[pl.ds(2 * g, 2), h, slot]
        pltpu.make_async_copy(part, part, recv_sem.at[slot, c]).wait()

    def frame_first(h):
        return (h % 2 == 0) | (h < 2)

    def own_sends(g, h, act):
        for k, df in enumerate((-1, 1)):
            @pl.when(has_frame[df])
            def _():
                act(remote(g, h, CENTRE, slot_of(-df, 0), df * ROWS, k))
        for k, dr in enumerate((-1, 1)):
            @pl.when(has_row[dr] & (frame_first(h) | ~crosses[dr]))
            def _():
                act(remote(g, h, CENTRE, slot_of(0, -dr), dr, 2 + k))

    def crossing_sends(g, h, act):
        for k, dr in enumerate((-1, 1)):
            @pl.when(crosses[dr] & ~frame_first(h))
            def _():
                act(remote(g, h, CENTRE, slot_of(0, -dr), dr, 2 + k))

    def later_sends(g, h, act, wait):
        kind = 4
        for df in (-1, 1):
            if wait:
                @pl.when(has_frame[df])
                def _():
                    wait_in(g, h, slot_of(df, 0))
            for dr in (-1, 1):
                @pl.when(has(df, dr) & (frame_first(h) | ~crosses[dr]))
                def _():
                    act(remote(g, h, slot_of(df, 0), slot_of(df, -dr), dr, kind))
                kind += 1
        if wait:
            @pl.when(middle & ~frame_first(h))
            def _():
                wait_in(g, h, CENTRE + row_way)
        for df in (-1, 1):
            @pl.when(has_frame[df] & middle & ~frame_first(h))
            def _():
                act(remote(g, h, CENTRE + row_way, (1 - df) * 3 + 1 + row_way, df * ROWS, kind))
            kind += 1

    def wait_rest(g, h):
        for dr in (-1, 1):
            @pl.when(has_row[dr] & (frame_first(h) | ~crosses[dr]))
            def _():
                wait_in(g, h, slot_of(0, dr))
        for df in (-1, 1):
            for dr in (-1, 1):
                @pl.when(has(df, dr))
                def _():
                    wait_in(g, h, slot_of(df, dr))

    def stat_copy(h, df, dr):
        dst = slot_of(-df, -dr)
        return pltpu.make_async_remote_copy(
            src_ref=stats.at[h, CENTRE], dst_ref=stats.at[h, dst],
            send_sem=stat_send.at[dst, h], recv_sem=stat_recv.at[dst, h],
            device_id={"seq": me + df * ROWS + dr}, device_id_type=MESH)

    def start(copy):
        copy.start()

    def wait_send(copy):
        copy.wait_send()

    for lead in range(OWN_AHEAD - PASS_AHEAD):
        own_sends(0, lead, start)
    bank[QUERIES, :, CENTRE] = jnp.transpose(q_ref[...], (1, 0, 2))
    bank[GRADS, :, CENTRE] = jnp.transpose(do_ref[...], (1, 0, 2))

    def cross(h, carry):
        crossing_sends(0, h, start)
        crossing_sends(1, h, start)
        return carry

    lax.fori_loop(0, heads, cross, 0)

    for df, dr in around:
        @pl.when(~has(df, dr))
        def _():
            slot = slot_of(df, dr)

            def clear(h, carry):
                for a in range(4):
                    bank[a, h, slot] = jnp.zeros((tok, dim), bank.dtype)
                stats[h, slot] = jnp.zeros(stats.shape[2:], stats.dtype)
                return carry

            lax.fori_loop(0, heads, clear, 0)

    tiles = kv_ref.shape[1]
    tile_ids = lax.broadcasted_iota(jnp.int32, (tiles, tiles), 0)
    listed = jnp.zeros((tiles, tiles), jnp.float32)
    for e in range(kv_ref.shape[0]):
        listed = jnp.where(kv_ref[e:e + 1, :] == tile_ids, 1.0, listed)
    lane = lax.broadcasted_iota(jnp.int32, (tiles, band), 1)
    slot_at = jnp.zeros_like(lane)
    for j in range(1, 9):
        slot_at += (lane >= j * tok).astype(jnp.int32)
    df_at = (lane >= 3 * tok).astype(jnp.int32) + (lane >= 6 * tok).astype(jnp.int32) - 1
    dr_at = slot_at - 3 * (df_at + 1) - 1
    col_at = lax.shift_right_logical(lane - slot_at * tok, 6)
    there = (frame + df_at >= 0) & (frame + df_at < frames) & (row + dr_at >= 0) & (row + dr_at < ROWS)
    tile_at = jnp.where(there, (me + df_at * ROWS + dr_at) * cols + col_at, -1)
    place = jnp.where(tile_at == lax.broadcasted_iota(jnp.int32, (tiles, band), 0), 1.0, 0.0)
    mine = jnp.where(
        lax.broadcasted_iota(jnp.int32, (8, tiles), 1) == me * cols + lax.broadcasted_iota(jnp.int32, (8, tiles), 0),
        1.0, 0.0)
    bias_q[...] = jnp.where(dot(dot(mine, listed, (1, 1)), place, (1, 0)) > 0.5, 0.0, HIDE)
    bias_k[...] = jnp.where(dot(dot(mine, listed, (1, 0)), place, (1, 0)) > 0.5, 0.0, HIDE)

    def rows_of(x, t):
        return x[t * TILE:(t + 1) * TILE]

    def queries_side(h):
        q, do = bank[QUERIES, h, CENTRE], bank[GRADS, h, CENTRE]
        k, v = bank[KEYS, h].reshape(band, dim), bank[VALUES, h].reshape(band, dim)
        s = dot(q, k, (1, 1))
        weights, tops, totals = [], [], []
        for t in range(cols):
            z = rows_of(s, t) * (scale * LOG2E) + bias_q[t:t + 1, :]
            top = jnp.max(z, axis=1, keepdims=True)
            w = jnp.exp2(z - top)
            weights.append(w)
            tops.append(top)
            totals.append(jnp.sum(w, axis=1, keepdims=True))
        w = jnp.concatenate(weights, axis=0)
        top, total = jnp.concatenate(tops, axis=0), jnp.concatenate(totals, axis=0)
        inv = 1.0 / total
        out = (dot(w.astype(jnp.bfloat16), v, (1, 0)) * inv).astype(jnp.bfloat16)
        out_ref[0, h] = out
        delta = jnp.sum(do.astype(jnp.float32) * out.astype(jnp.float32), axis=1, keepdims=True)
        dw = dot(do, v, (1, 1))
        ds = (w * (dw - delta) * (inv * scale)).astype(jnp.bfloat16)
        out_ref[1, h] = dot(ds, k, (1, 0)).astype(jnp.bfloat16)
        lse = top + jnp.log(total) * LOG2E
        wide = jnp.where(lax.broadcasted_iota(jnp.int32, (tok, 128), 1) == 0, lse, delta)
        turned = jnp.transpose(wide)
        stats[h, CENTRE, :, 0:tok] = turned[0:2]

    def keys_side(h):
        k, v = bank[KEYS, h, CENTRE], bank[VALUES, h, CENTRE]
        q, do = bank[QUERIES, h].reshape(band, dim), bank[GRADS, h].reshape(band, dim)
        s = dot(k, q, (1, 1))
        st = jnp.concatenate([stats[h, j, :, 0:tok] for j in range(9)], axis=1)
        lse, delta = st[0:1], st[1:2]
        w = jnp.concatenate(
            [jnp.exp2(rows_of(s, t) * (scale * LOG2E) + (bias_k[t:t + 1, :] - lse)) for t in range(cols)], axis=0)
        out_ref[3, h] = dot(w.astype(jnp.bfloat16), do, (1, 0)).astype(jnp.bfloat16)
        dw = dot(v, do, (1, 1))
        ds = (w * ((dw - delta) * scale)).astype(jnp.bfloat16)
        out_ref[2, h] = dot(ds, q, (1, 0)).astype(jnp.bfloat16)

    def step(t, carry):
        def at(lag):
            h = t - lag
            if lag > 0:
                return h, (h >= 0) & (h < heads)
            return h, h < heads

        h_pass, turn = at(0)
        @pl.when(turn)
        def _():
            later_sends(0, h_pass, start, True)

        h_pass_late, turn = at(LAG)
        @pl.when(turn)
        def _():
            later_sends(1, h_pass_late, start, True)

        h_own, turn = at(PASS_AHEAD - OWN_AHEAD)
        @pl.when(turn)
        def _():
            own_sends(0, h_own, start)

        h_own_late, turn = at(PASS_AHEAD - OWN_AHEAD + LAG)
        @pl.when(turn)
        def _():
            own_sends(1, h_own_late, start)

        i, turn = at(PASS_AHEAD)
        @pl.when(turn)
        def _():
            wait_rest(0, i)
            queries_side(i)
            for df, dr in around:
                @pl.when(has(df, dr))
                def _():
                    stat_copy(i, df, dr).start()

        h, turn = at(PASS_AHEAD + LAG)
        @pl.when(turn)
        def _():
            wait_rest(1, h)
            for df, dr in around:
                @pl.when(has(df, dr))
                def _():
                    slot = slot_of(df, dr)
                    part = stats.at[h, slot]
                    pltpu.make_async_copy(part, part, stat_recv.at[slot, h]).wait()
            keys_side(h)

        return carry

    lax.fori_loop(0, heads + LAG + PASS_AHEAD, step, 0)

    def finish(h, carry):
        for g in range(2):
            own_sends(g, h, wait_send)
            crossing_sends(g, h, wait_send)
            later_sends(g, h, wait_send, False)
        for df, dr in around:
            @pl.when(has(df, dr))
            def _():
                stat_copy(h, df, dr).wait_send()
        return carry

    lax.fori_loop(0, heads, finish, 0)


def by_token(in_ref, *out_refs):
    for a, ref in enumerate(out_refs):
        ref[...] = jnp.transpose(in_ref[a], (1, 0, 2))


def on_device(devices, queries, key_rows, value_rows, grad_out, kv_tiles, counts):
    tok, heads, dim = queries.shape
    out = pl.pallas_call(
        functools.partial(kernel, devices),
        out_shape=jax.ShapeDtypeStruct((4, heads, tok, dim), jnp.bfloat16),
        in_specs=[pl.BlockSpec(memory_space=pltpu.VMEM)] * 5,
        out_specs=pl.BlockSpec(memory_space=pltpu.VMEM),
        scratch_shapes=[
            pltpu.VMEM((4, heads, 9, tok, dim), jnp.bfloat16),
            pltpu.VMEM((heads, 9, 2, 256), jnp.float32),
            pltpu.VMEM((8, 9 * tok), jnp.float32),
            pltpu.VMEM((8, 9 * tok), jnp.float32),
            pltpu.SemaphoreType.DMA((10, 2 * heads)),
            pltpu.SemaphoreType.DMA((9, 2 * heads)),
            pltpu.SemaphoreType.DMA((9, heads)),
            pltpu.SemaphoreType.DMA((9, heads)),
        ],
        compiler_params=pltpu.CompilerParams(collective_id=0, has_side_effects=True, vmem_limit_bytes=56 * 2**20),
    )(key_rows, value_rows, queries, grad_out, kv_tiles.T)
    return tuple(pl.pallas_call(
        by_token,
        out_shape=[jax.ShapeDtypeStruct(queries.shape, queries.dtype)] * 4,
        in_specs=[pl.BlockSpec(memory_space=pltpu.VMEM)],
        out_specs=[pl.BlockSpec(memory_space=pltpu.VMEM)] * 4,
    )(out))


def solution(mesh):
    rows = P(("parts", "seq"), None, None)
    return jax.shard_map(
        functools.partial(on_device, mesh.shape["seq"]),
        mesh=mesh,
        in_specs=(rows, rows, rows, rows, P("parts", None), P("parts")),
        out_specs=(rows, rows, rows, rows),
        check_vma=False,
    )
```
